32 devices in a mesh: req: 16 (over z, x, core), blk: 2 (over y).
Axes of the slice: x: 2, y: 2, z: 4, core: 2. Of those that a mesh axis runs over, the one named last changes fastest.
Arguments:
- queries: bfloat16 [32, 64, 2048], P('req', 'blk'), may hold values from -5 to 5
- cache_keys: bfloat16 [32, 1024, 2048], P('req', 'blk'), may hold values from -5 to 5
- cache_values: bfloat16 [32, 1024, 2048], P('req', 'blk'), may hold values from -6 to 6
- draft_keys: bfloat16 [32, 64, 2048], P('req', 'blk'), may hold values from -6 to 6
- draft_values: bfloat16 [32, 64, 2048], P('req', 'blk'), may hold values from -6 to 6
- parents: int32 [32, 64], P('req'), may hold values from -1 to 62, as said below
- lengths: int32 [32], P('req'), may hold values from 2 to 1024
- out_weight: bfloat16 [2048, 4096], P('req'), may hold values from -0.125 to 0.125
Outputs:
- mixed: bfloat16 [32, 64, 4096], P('req', 'blk')
The draws below stay inside these ranges and needn't reach their ends.
Inputs may be any that keep to these rules, and one draw needn't show every extreme that they name: parents[r, t] is below t; parents[r, 0] = -1 marks the root, which follows the cache.
All inputs are finite; a program needn't handle non-finite values.
Results may differ from the reference program's by a relative error of at most 0.0054.
Values may be sent and summed in bfloat16 or wider, within the bound.
A program may use at most 128 MiB of HBM per device.

```python
import jax
import jax.numpy as jnp
from jax import lax

D = 4096
HEAD = 128
HEADS = 16
ATT = 2048
TREE = 64
REQS = 32
CACHE = 1024


def joint_fields(key):
    key_q, key_k = jax.random.split(jax.random.fold_in(key, 77), 2)
    query = jnp.clip(jax.random.normal(key_q, (REQS, TREE, ATT), jnp.float32), -5.0, 5.0)
    cache = jnp.clip(jax.random.normal(key_k, (REQS, CACHE, ATT), jnp.float32), -5.0, 5.0)
    return (query, cache)


def draw_queries(key, part):
    return joint_fields(key)[0].astype(jnp.bfloat16)


def draw_cache_keys(key, part):
    return joint_fields(key)[1].astype(jnp.bfloat16)


def draw_parents(key, part):
    index = jnp.arange(TREE, dtype=jnp.int32)[None, :]
    upper = jnp.broadcast_to(jnp.maximum(index, 1), (REQS, TREE))
    picks = jax.random.randint(key, (REQS, TREE), 0, upper, dtype=jnp.int32)
    picks = jnp.where(index == 0, -1, picks)
    picks = jnp.where(index == TREE - 1, TREE - 2, picks)
    return picks.astype(jnp.int32)


def draw_lengths(key, part):
    key_a, key_b = jax.random.split(key)
    first = jax.random.randint(key_a, (REQS,), 2, CACHE + 1, dtype=jnp.int32)
    second = jax.random.randint(key_b, (REQS,), 2, CACHE + 1, dtype=jnp.int32)
    result = jnp.minimum(first, second)
    result = result.at[0].set(CACHE).at[1].set(2)
    return result.astype(jnp.int32)


def shard_levels(key, shape, pieces, smallest, top_value):
    def one(axis_at, shards_of):
        draws = jax.random.uniform(jax.random.fold_in(jax.random.fold_in(key, 6), axis_at), (shards_of,), jnp.float32, smallest / len(pieces), top_value / len(pieces))
        return jnp.repeat(jnp.exp(draws), shape[axis_at] // shards_of).reshape((-1,) + (1,) * (len(shape) - axis_at - 1))

    loudness = one(*pieces[0])
    for cut in pieces[1:]:
        loudness = loudness * one(*cut)
    return loudness


def bell_draw(key, shape, deviation, reach, cuts=(), kind=jnp.bfloat16):
    entries = deviation * jax.random.normal(key, shape, jnp.float32)
    if cuts:
        entries = entries * shard_levels(key, shape, cuts, -0.22, 0.18)
    return jnp.clip(entries, -reach, reach).astype(kind)


def setup_inputs(seed: int = 0) -> dict:
    key_list = jax.random.split(jax.random.key(seed), 9)
    queries = draw_queries(jax.random.fold_in(key_list[8], 71), 0)
    cache_keys = draw_cache_keys(jax.random.fold_in(key_list[8], 71), 0)
    cache_values = bell_draw(key_list[2], (REQS, CACHE, ATT), 1.0, 6.0, ((0, 16), (1, 2)))
    draft_keys = bell_draw(key_list[3], (REQS, TREE, ATT), 1.0, 6.0, ((0, 16), (1, 2)))
    draft_values = bell_draw(key_list[4], (REQS, TREE, ATT), 1.0, 6.0, ((0, 16), (1, 2)))
    parents = draw_parents(jax.random.fold_in(key_list[8], 71), 0)
    lengths = draw_lengths(jax.random.fold_in(key_list[8], 71), 0)
    out_weight = bell_draw(key_list[7], (ATT, D), ATT ** -0.5, 0.125, ((0, 16),))
    return {"queries": queries, "cache_keys": cache_keys, "cache_values": cache_values, "draft_keys": draft_keys, "draft_values": draft_values, "parents": parents, "lengths": lengths, "out_weight": out_weight}


def ancestors(parent_row):
    index = jnp.arange(TREE)
    links = (parent_row[:, None] == index[None, :]).astype(jnp.float32)
    links = links + (index[:, None] == index[None, :]).astype(jnp.float32)
    for _ in range(TREE.bit_length()):
        links = jnp.minimum(jnp.dot(links, links, precision=lax.Precision.HIGHEST, preferred_element_type=jnp.float32), 1.0)
    return links > 0.5


def one_request(items):
    query, cache_k, cache_v, draft_k, draft_v, parent_row, length = items
    scale = HEAD ** -0.5
    qf = query.astype(jnp.float32).reshape(TREE, HEADS, HEAD)
    keys = jnp.concatenate([cache_k, draft_k], axis=0).astype(jnp.float32).reshape(-1, HEADS, HEAD)
    values = jnp.concatenate([cache_v, draft_v], axis=0).astype(jnp.float32).reshape(-1, HEADS, HEAD)
    scores = jnp.einsum("the,khe->htk", qf, keys) * scale
    cache_seen = jnp.broadcast_to((jnp.arange(CACHE) < length)[None, :], (TREE, CACHE))
    seen = jnp.concatenate([cache_seen, ancestors(parent_row)], axis=1)[None]
    scores = jnp.where(seen, scores, -1e30)
    row_max = jnp.max(scores, axis=-1)
    weights = jnp.where(seen, jnp.exp(scores - row_max[..., None]), 0.0)
    totals = jnp.sum(weights, axis=-1)
    rounded = lax.optimization_barrier(weights.astype(jnp.bfloat16)).astype(jnp.float32)
    numer = jnp.einsum("htk,khe->the", rounded, values)
    attended = numer / jnp.transpose(totals)[..., None]
    return attended.reshape(TREE, ATT).astype(jnp.bfloat16)


def reference(queries, cache_keys, cache_values, draft_keys, draft_values, parents, lengths, out_weight):
    attended = lax.map(one_request, (queries, cache_keys, cache_values, draft_keys, draft_values, parents, lengths))
    mixed = jnp.dot(attended.reshape(-1, ATT), out_weight, preferred_element_type=jnp.float32)
    return mixed.astype(jnp.bfloat16).reshape(REQS, TREE, D)
```

```python
import functools

import jax
import jax.numpy as jnp
from jax import lax
from jax.experimental import pallas as pl
from jax.experimental.pallas import tpu as pltpu
from jax.sharding import PartitionSpec as P

HEAD = 128
HEADS = 16
LOW = 4
PARTS = 4
CHUNK = 256
FIRST = 14
NEAR = 2
ORDER = ((0, 1), (1, 1), (0, 2), (0, 3), (1, 2), (1, 3), )
STEPS = ((0, 1), (1, 1), (0, 2), (0, 3), (1, 2), (1, 3), )
PASSED = (0, 1, )
SCHEDULE = ("a00", "w", "w", "a01", "e0", "w", "w", "a10", "a11", "e1", "w", "w", "m0", "a20", "a21", "e2", "m1", "w", "a30", "a31", "e3", "w", "m2", "z0", "w", "m3", "w", "f0", "z1", "w", "w", "w", "f1", "z2", "w", "z3", "p00", "p01", "p10", "p11",)
MESH = pl.DeviceIdType.MESH
NEG = -1e30
COEF = HEAD**-0.5 * 1.4426950408889634


def flip(value, bits):
    out = value
    bit = 1
    while bit <= bits:
        if bits & bit:
            out = out + bit - 2 * bit * ((value // bit) % 2)
        bit *= 2
    return out


def kernel(
    nreq, nblk,
    q_hbm, ck_hbm, cv_hbm, dk_hbm, dv_hbm, par_ref, len_ref, w_hbm,
    out_hbm,
    qbuf, kbuf, vbuf, dkbuf, dvbuf, vtmp, vis, nown, nsend, nrecv, stat, ssend, srecv, abuf, wbuf, obuf,
    kv_sem, d_sem, q_send, q_recv, n_send, n_recv, s_send, s_recv,
    wz_send, wx_send, w_recv, known, a_send, a_recv, o_send, o_recv,
):
    batch, own, width = q_hbm.shape
    keys = ck_hbm.shape[1]
    tree = own * nblk
    rows = batch * own
    rows_w, model = w_hbm.shape
    ncols = model // (4 * nblk)
    chunk = min(CHUNK, ncols)
    pieces = ncols // chunk
    depth = nreq // LOW
    req, blk = lax.axis_index("req"), lax.axis_index("blk")
    z, x, c = req // LOW, (req // 2) % 2, req % 2

    def at(zz, xx, cc):
        return zz * LOW + xx * 2 + cc

    def slot(zr, cr, yr):
        return (zr * 2 + cr) * nblk + yr

    def member(zr, cr, yr):
        return (at(flip(z, zr), x, flip(c, cr)), lax.rem(blk + yr, nblk))

    def columns(zz, yy, cc, n):
        index = ((zz % 2) * nblk + yy) * 2 + cc
        return pl.ds(pl.multiple_of(index * ncols + n * chunk, chunk), chunk)

    def back(yr):
        return (nblk - yr) % nblk

    part = width // PARTS
    pcols = [pl.ds(p * part, part) for p in range(PARTS)]

    locals_d = [
        pltpu.make_async_copy(q_hbm, qbuf.at[0], d_sem.at[0]),
        pltpu.make_async_copy(dk_hbm, dkbuf, d_sem.at[1]),
        pltpu.make_async_copy(dv_hbm, dvbuf, d_sem.at[2]),
    ]
    for copy in locals_d:
        copy.start()
    kv = []
    for p in range(PARTS):
        pair = (
            pltpu.make_async_copy(ck_hbm.at[:, :, pcols[p]], kbuf.at[:, :, pcols[p]], kv_sem.at[0, p]),
            pltpu.make_async_copy(cv_hbm.at[:, :, pcols[p]], vbuf.at[:, :, pcols[p]], kv_sem.at[1, p]),
        )
        for copy in pair:
            copy.start()
        kv.append(pair)

    xpeer = (at(z, 1 - x, c), blk)
    line = [(d, e) for d in range(depth) for e in range(2) if d or e]
    peers = [xpeer, (at(z, x, 1 - c), blk)] + [member(0, 0, b) for b in range(1, nblk)]
    barrier = pltpu.get_barrier_semaphore()

    def beside(act):
        for side, exists in ((z - 1, z > 0), (z + 1, z < depth - 1)):
            @pl.when(exists)
            def _():
                act(side)

    ends = (z == 0).astype(jnp.int32) + (z == depth - 1).astype(jnp.int32)
    for peer in peers:
        pl.semaphore_signal(barrier, inc=1, device_id=peer, device_id_type=MESH)

    def greet(side):
        for cc in range(2):
            pl.semaphore_signal(barrier, inc=1, device_id=(at(side, x, cc), blk), device_id_type=MESH)

    beside(greet)
    pl.semaphore_wait(barrier, len(peers) + 4 - 2 * ends)

    def tell(s):
        def signal(side):
            pl.semaphore_signal(known.at[s], inc=1, device_id=(at(side, x, c), blk), device_id_type=MESH)

        beside(signal)

    def stage(s):
        pl.semaphore_wait(known.at[s], 2 - ends)
        if s + 1 < depth - 2:
            tell(s + 1)

    def remote(src, dst, send, recv, peer):
        return pltpu.make_async_remote_copy(
            src_ref=src, dst_ref=dst, send_sem=send, recv_sem=recv, device_id=peer, device_id_type=MESH
        )

    sent = []

    def send(*what):
        copy = remote(*what)
        copy.start()
        sent.append(copy)

    def await_recv(dst, sem):
        remote(dst, dst, wx_send.at[0, 0, 0], sem, xpeer).wait_recv()

    for p in range(PARTS):
        for b in range(1, nblk):
            send(
                q_hbm.at[:, :, pcols[p]], qbuf.at[back(b), :, :, pcols[p]],
                q_send.at[p, b], q_recv.at[p, back(b)], member(0, 0, b),
            )

    def wdst(n, source):
        return wbuf.at[pl.ds(pl.multiple_of(source * rows_w, rows_w), rows_w), pl.ds(n * chunk, chunk)]

    def wsrc(n, zz, cc):
        return w_hbm.at[:, columns(zz, blk, cc, n)]

    own_w = []
    for n in range(pieces):
        send(wsrc(n, z, c), wdst(n, req), wx_send.at[n, 0, 0], w_recv.at[n, req], xpeer)
        copy = pltpu.make_async_copy(wsrc(n, z, c), wdst(n, req), w_recv.at[n, req])
        copy.start()
        own_w.append(copy)

    rest = [(n, d) for n, d in ORDER if n < pieces and d < depth]
    rest += [(n, d) for n in range(pieces) for d in range(1, depth) if (n, d) not in rest]
    puts = [(n, 0, 1) for n in range(pieces)] + [(n, d, e) for n, d in rest for e in range(2)]
    order = [(n, d) for n, d in STEPS if n < pieces and d < depth]
    order += [pair for pair in rest if pair not in order]
    steps = [(n, 0, 1) for n in range(pieces)] + [(n, d, e) for n, d in order for e in range(2)]
    done, gone = [0], [0]

    def pump(upto):
        while gone[0] < min(upto, len(puts)):
            n, d, e = puts[gone[0]]
            gone[0] += 1
            zz, cc = flip(z, d), flip(c, e)
            send(wsrc(n, zz, cc), wdst(n, req), wz_send.at[n, d, e], w_recv.at[n, req], (at(zz, x, cc), blk))

    pump(pieces + 2 * sum(d == 1 for _, d in rest[:NEAR]))
    if depth > 2:
        tell(0)

    def forward(upto):
        while done[0] < min(upto, len(steps)):
            n, d, e = steps[done[0]]
            done[0] += 1
            source = at(flip(z, d), x, flip(c, e))
            await_recv(wdst(n, source), w_recv.at[n, source])
            send(wdst(n, source), wdst(n, source), wx_send.at[n, d, e], w_recv.at[n, source], xpeer)

    row_i = lax.broadcasted_iota(jnp.int32, (tree, tree), 0)
    col_i = lax.broadcasted_iota(jnp.int32, (tree, tree), 1)
    pick = (
        lax.broadcasted_iota(jnp.int32, (tree, own), 0)
        == lax.broadcasted_iota(jnp.int32, (tree, own), 1) + blk * own
    ).astype(jnp.float32).astype(jnp.bfloat16)
    for r in range(batch):
        links = ((par_ref[pl.ds(r, 1), :] == row_i) | (row_i == col_i)).astype(jnp.float32)
        for _ in range((tree - 1).bit_length()):
            half = links.astype(jnp.bfloat16)
            links = jnp.minimum(jnp.dot(half, half, preferred_element_type=jnp.float32), 1.0)
        vtmp[r] = lax.dot_general(
            links.astype(jnp.bfloat16), pick, (((0,), (0,)), ((), ())),
            preferred_element_type=jnp.float32,
        )
    for r in range(batch):
        for b in range(nblk):
            there = pl.ds(pl.multiple_of(lax.rem(blk + b, nblk) * own, own), own)
            vis[r, pl.ds(b * own, own)] = vtmp[r, there]
    stat[...] = jnp.zeros_like(stat)
    for s in range(depth - 2):
        stage(s)
    pump(FIRST)

    at_key = lax.broadcasted_iota(jnp.int32, (1, keys), 1) + blk * keys
    seen = [at_key < len_ref[r] for r in range(batch)]
    lane = lax.broadcasted_iota(jnp.int32, (rows, 128), 1)
    per_p = HEADS // PARTS

    def head(p, i):
        cols = pl.ds((p * per_p + i) * HEAD, HEAD)
        stats = []
        for r in range(batch):
            tokens = [qbuf[b, r, :, cols] for b in range(nblk)]
            if own % 16:
                q = jnp.concatenate([piece.astype(jnp.float32) for piece in tokens], axis=0)
                q = q.astype(jnp.bfloat16)
            else:
                q = jnp.concatenate(tokens, axis=0)
            dims = (((1,), (1,)), ((), ()))
            s1 = lax.dot_general(q, kbuf[r, :, cols], dims, preferred_element_type=jnp.float32)
            s2 = lax.dot_general(q, dkbuf[r, :, cols], dims, preferred_element_type=jnp.float32)
            s1 = jnp.where(seen[r], s1, NEG)
            s2 = jnp.where(vis[r] > 0.5, s2, NEG)
            top = jnp.maximum(
                jnp.max(s1, axis=-1, keepdims=True), jnp.max(s2, axis=-1, keepdims=True)
            )
            top = jnp.maximum(top, 0.1 * NEG)
            p1 = jnp.exp2((s1 - top) * COEF)
            p2 = jnp.exp2((s2 - top) * COEF)
            total = jnp.sum(p1, axis=-1, keepdims=True) + jnp.sum(p2, axis=-1, keepdims=True)
            numer = jnp.dot(
                p1.astype(jnp.bfloat16), vbuf[r, :, cols], preferred_element_type=jnp.float32
            ) + jnp.dot(
                p2.astype(jnp.bfloat16), dvbuf[r, :, cols], preferred_element_type=jnp.float32
            )
            stats.append((top, total, numer))
        for b in range(nblk):
            of = slice(b * own, (b + 1) * own)
            top, total, numer = (
                jnp.concatenate([s[j][of] for s in stats], axis=0) for j in range(3)
            )
            nown[b, :, cols] = numer
            nsend[b, :, cols] = numer.astype(jnp.bfloat16)
            at_rows = pl.ds(b * rows, rows)
            stat[p, at_rows] = jnp.where(
                lane == i, top, jnp.where(lane == i + per_p, total, stat[p, at_rows])
            )

    def attend(p, half):
        if half == 0:
            for copy in kv[p]:
                copy.wait()
            for b in range(1, nblk):
                await_recv(qbuf.at[b, :, :, pcols[p]], q_recv.at[p, b])
        for i in range(half * per_p // 2, (half + 1) * per_p // 2):
            head(p, i)

    def exchange(p):
        ssend[p] = stat[p].T[: 2 * per_p]
        for b in range(1, nblk):
            send(
                nsend.at[:, :, pcols[p]], nrecv.at[back(b), :, :, pcols[p]],
                n_send.at[p, b], n_recv.at[p, back(b)], member(0, 0, b),
            )
            send(ssend.at[p], srecv.at[p, back(b)], s_send.at[p, b], s_recv.at[p, back(b)], member(0, 0, b))

    def piece(zr, cr, yr, p):
        if yr is None:
            return abuf.at[pl.ds(slot(zr, cr, 0), nblk), :, pcols[p]]
        return abuf.at[slot(zr, cr, yr), :, pcols[p]]

    def sem(zr, cr, yr, p):
        return a_recv.at[p, slot(zr, cr, yr or 0)]

    def share(p, mine, there, to, s):
        send(piece(*mine, p), piece(*there, p), a_send.at[p, s], sem(*there, p), member(*to))

    def merge(p):
        stats = [stat[p]]
        for a in range(1, nblk):
            await_recv(nrecv.at[a, :, :, pcols[p]], n_recv.at[p, a])
            await_recv(srecv.at[p, a], s_recv.at[p, a])
            stats.append(srecv[p, a].T)
        for b in range(nblk):
            places = [(b - a) % nblk for a in range(nblk)]
            own_stats = [s[k * rows : (k + 1) * rows] for s, k in zip(stats, places)]
            tops = [s[:, :per_p] for s in own_stats]
            sums = [s[:, per_p : 2 * per_p] for s in own_stats]
            top = functools.reduce(jnp.maximum, tops)
            factors = [jnp.exp2((t - top) * COEF) for t in tops]
            total = sum(s * f for s, f in zip(sums, factors))
            factors = [f / total for f in factors]
            for i in range(per_p):
                cols = pl.ds((p * per_p + i) * HEAD, HEAD)
                row = nown[b, :, cols] * factors[0][:, i : i + 1]
                for a in range(1, nblk):
                    row = row + nrecv[a, places[a], :, cols].astype(jnp.float32) * factors[a][:, i : i + 1]
                abuf[b, :, cols] = row.astype(jnp.bfloat16)
            if b == 0 and p in PASSED:
                share(p, (0, 0, 0), (1, 0, 0), (1, 0, 0), 0)
        if p not in PASSED:
            share(p, (0, 0, None), (1, 0, None), (1, 0, 0), 0)
        share(p, (0, 0, None), (0, 1, None), (0, 1, 0), 1)

    def near(p):
        yr = 0 if p in PASSED else None
        await_recv(piece(1, 0, yr, p), sem(1, 0, yr, p))
        if p in PASSED:
            for b in range(1, nblk):
                share(p, (1, 0, 0), (1, 0, back(b)), (0, 0, b), 2 + b)
        share(p, (1, 0, yr), (1, 1, yr), (0, 1, 0), 2)

    def far(p):
        if p in PASSED:
            for b in range(1, nblk):
                await_recv(piece(1, 0, b, p), sem(1, 0, b, p))
                share(p, (1, 0, b), (1, 1, b), (0, 1, 0), 2 + nblk + b)

    for copy in locals_d:
        copy.wait()

    ymembers = [(cr, yr) for cr in range(2) for yr in range(nblk)]

    def project(n, zr):
        cols = pl.ds(n * chunk, chunk)
        out = jnp.dot(
            abuf[pl.ds(zr * 2 * nblk, 2 * nblk)].reshape(2 * nblk * rows, width), wbuf[:, cols],
            preferred_element_type=jnp.float32,
        )
        obuf[pl.ds(zr * 2 * nblk, 2 * nblk), :, :, cols] = out.reshape(2 * nblk, batch, own, chunk).astype(jnp.bfloat16)
        there = columns(z, blk, c, n)
        for cr, yr in ymembers:
            k = slot(zr, cr, yr)
            if k:
                to = slot(zr, cr, back(yr))
                send(
                    obuf.at[k, :, :, cols], out_hbm.at[:, :, there],
                    o_send.at[n, k], o_recv.at[n, to], member(zr, cr, yr),
                )
            else:
                home = pltpu.make_async_copy(obuf.at[0, :, :, cols], out_hbm.at[:, :, there], o_recv.at[n, 0])
                home.start()
                homes.append(home)

    homes = []
    ready = set()

    def finish(n, zr):
        if n >= pieces:
            return
        if zr == 0:
            pump(len(puts))
            forward(1 + max(k for k, step in enumerate(steps) if step[0] == n))
            own_w[n].wait()
            for d in range(depth):
                for e in range(2):
                    source = at(flip(z, d), 1 - x, flip(c, e))
                    await_recv(wdst(n, source), w_recv.at[n, source])
        if n == 0:
            for p in range(PARTS):
                for yr in range(nblk) if zr and p in PASSED else (None,):
                    await_recv(piece(zr, 1, yr, p), sem(zr, 1, yr, p))
        project(n, zr)

    for op in SCHEDULE:
        kind, a, b = op[0], int(op[1:] or 0), int(op[-1:] if op[1:] else 0)
        if kind == "a":
            attend(a // 10, b)
        elif kind == "e":
            exchange(a)
        elif kind == "m":
            merge(a)
        elif kind == "z":
            near(a)
        elif kind == "f":
            far(a)
        elif kind == "s":
            pump(gone[0] + 1)
        elif kind == "w":
            forward(done[0] + 1)
        else:
            finish(a // 10, b)
    for n in range(pieces):
        homes[n].wait()
        for zr in range(2):
            for cr, yr in ymembers:
                k = slot(zr, cr, yr)
                if k:
                    there = columns(flip(z, zr), lax.rem(blk + yr, nblk), flip(c, cr), n)
                    await_recv(out_hbm.at[:, :, there], o_recv.at[n, k])
    for copy in sent:
        copy.wait_send()


def shards(nreq, nblk, queries, cache_keys, cache_values, draft_keys, draft_values, parents, lengths, out_weight):
    batch, own, width = queries.shape
    keys = cache_keys.shape[1]
    tree = own * nblk
    rows = batch * own
    rows_w, model = out_weight.shape
    group = 4 * nblk
    ncols = model // group
    pieces = ncols // min(CHUNK, ncols)
    depth = nreq // LOW
    bf16, f32 = jnp.bfloat16, jnp.float32
    dma = pltpu.SemaphoreType.DMA
    hbm = pl.BlockSpec(memory_space=pltpu.HBM)
    vmem = pl.BlockSpec(memory_space=pltpu.VMEM)
    smem = pl.BlockSpec(memory_space=pltpu.SMEM)
    return pl.pallas_call(
        functools.partial(kernel, nreq, nblk),
        out_shape=jax.ShapeDtypeStruct((batch, own, model), bf16),
        in_specs=[hbm, hbm, hbm, hbm, hbm, vmem, smem, hbm],
        out_specs=hbm,
        scratch_shapes=[
            pltpu.VMEM((nblk, batch, own, width), bf16),
            pltpu.VMEM((batch, keys, width), bf16),
            pltpu.VMEM((batch, keys, width), bf16),
            pltpu.VMEM((batch, own, width), bf16),
            pltpu.VMEM((batch, own, width), bf16),
            pltpu.VMEM((batch, tree, own), f32),
            pltpu.VMEM((batch, tree, own), f32),
            pltpu.VMEM((nblk, rows, width), f32),
            pltpu.VMEM((nblk, rows, width), bf16),
            pltpu.VMEM((nblk, nblk, rows, width), bf16),
            pltpu.VMEM((PARTS, batch * tree, 128), f32),
            pltpu.VMEM((PARTS, 2 * HEADS // PARTS, batch * tree), f32),
            pltpu.VMEM((PARTS, nblk, 2 * HEADS // PARTS, batch * tree), f32),
            pltpu.VMEM((group, rows, width), bf16),
            pltpu.VMEM((rows_w * nreq, ncols), bf16),
            pltpu.VMEM((group, batch, own, ncols), bf16),
            dma((2, PARTS)),
            dma((3,)),
            dma((PARTS, nblk)),
            dma((PARTS, nblk)),
            dma((PARTS, nblk)),
            dma((PARTS, nblk)),
            dma((PARTS, nblk)),
            dma((PARTS, nblk)),
            dma((pieces, depth, 2)),
            dma((pieces, depth, 2)),
            dma((pieces, nreq)),
            pltpu.SemaphoreType.REGULAR((depth - 2,)),
            dma((PARTS, 2 + 4 * nblk)),
            dma((PARTS, group)),
            dma((pieces, group)),
            dma((pieces, group)),
        ],
        compiler_params=pltpu.CompilerParams(
            collective_id=0, has_side_effects=True, vmem_limit_bytes=58 * 1024 * 1024
        ),
    )(queries, cache_keys, cache_values, draft_keys, draft_values, parents, lengths, out_weight)


def solution(mesh):
    in_specs = (
        P("req", "blk", None),
        P("req", "blk", None),
        P("req", "blk", None),
        P("req", "blk", None),
        P("req", "blk", None),
        P("req", None),
        P("req"),
        P("req", None),
    )
    out_specs = P("req", "blk", None)
    body = functools.partial(shards, mesh.shape["req"], mesh.shape["blk"])
    return jax.shard_map(body, mesh=mesh, in_specs=in_specs, out_specs=out_specs, check_vma=False)
```

```python
import functools

import jax
import jax.numpy as jnp
from jax import lax
from jax.experimental import pallas as pl
from jax.experimental.pallas import tpu as pltpu
from jax.sharding import PartitionSpec as P

HEAD = 128
HEADS = 16
LOW = 4
PARTS = 4
CHUNK = 256
FIRST = 14
NEAR = 2
ORDER = ((0, 1), (1, 1), (0, 2), (0, 3), (1, 2), (1, 3), )
STEPS = ((0, 1), (1, 1), (0, 2), (0, 3), (1, 2), (1, 3), )
PASSED = (0, 1, )
SCHEDULE = ("a00", "a01", "w", "w", "e0", "a10", "a11", "w", "w", "e1", "w", "w", "m0", "a20", "a21", "e2", "m1", "w", "a30", "a31", "e3", "w", "m2", "z0", "w", "m3", "w", "z1", "w", "w", "f0", "z2", "w", "f1", "w", "z3", "p00", "p01", "p10", "p11",)
MESH = pl.DeviceIdType.MESH
NEG = -1e30
COEF = HEAD**-0.5 * 1.4426950408889634


def flip(value, bits):
    out = value
    bit = 1
    while bit <= bits:
        if bits & bit:
            out = out + bit - 2 * bit * ((value // bit) % 2)
        bit *= 2
    return out


def kernel(
    nreq, nblk,
    q_hbm, ck_hbm, cv_hbm, dk_hbm, dv_hbm, par_ref, len_ref, w_hbm,
    out_hbm,
    qbuf, kbuf, vbuf, dkbuf, dvbuf, vtmp, vis, nown, nsend, nrecv, stat, ssend, srecv, abuf, wbuf, obuf,
    kv_sem, d_sem, q_send, q_recv, n_send, n_recv, s_send, s_recv,
    wz_send, wx_send, w_recv, known, a_send, a_recv, o_send, o_recv,
):
    batch, own, width = q_hbm.shape
    keys = ck_hbm.shape[1]
    tree = own * nblk
    rows = batch * own
    rows_w, model = w_hbm.shape
    ncols = model // (4 * nblk)
    chunk = min(CHUNK, ncols)
    pieces = ncols // chunk
    depth = nreq // LOW
    req, blk = lax.axis_index("req"), lax.axis_index("blk")
    z, x, c = req // LOW, (req // 2) % 2, req % 2

    def at(zz, xx, cc):
        return zz * LOW + xx * 2 + cc

    def slot(zr, cr, yr):
        return (zr * 2 + cr) * nblk + yr

    def member(zr, cr, yr):
        return (at(flip(z, zr), x, flip(c, cr)), lax.rem(blk + yr, nblk))

    def columns(zz, yy, cc, n):
        index = ((zz % 2) * nblk + yy) * 2 + cc
        return pl.ds(pl.multiple_of(index * ncols + n * chunk, chunk), chunk)

    def back(yr):
        return (nblk - yr) % nblk

    part = width // PARTS
    pcols = [pl.ds(p * part, part) for p in range(PARTS)]

    locals_d = [
        pltpu.make_async_copy(q_hbm, qbuf.at[0], d_sem.at[0]),
        pltpu.make_async_copy(dk_hbm, dkbuf, d_sem.at[1]),
        pltpu.make_async_copy(dv_hbm, dvbuf, d_sem.at[2]),
    ]
    for copy in locals_d:
        copy.start()
    kv = []
    for p in range(PARTS):
        pair = (
            pltpu.make_async_copy(ck_hbm.at[:, :, pcols[p]], kbuf.at[:, :, pcols[p]], kv_sem.at[0, p]),
            pltpu.make_async_copy(cv_hbm.at[:, :, pcols[p]], vbuf.at[:, :, pcols[p]], kv_sem.at[1, p]),
        )
        for copy in pair:
            copy.start()
        kv.append(pair)

    xpeer = (at(z, 1 - x, c), blk)
    line = [(d, e) for d in range(depth) for e in range(2) if d or e]
    peers = [xpeer, (at(z, x, 1 - c), blk)] + [member(0, 0, b) for b in range(1, nblk)]
    barrier = pltpu.get_barrier_semaphore()

    def beside(act):
        for side, exists in ((z - 1, z > 0), (z + 1, z < depth - 1)):
            @pl.when(exists)
            def _():
                act(side)

    ends = (z == 0).astype(jnp.int32) + (z == depth - 1).astype(jnp.int32)
    for peer in peers:
        pl.semaphore_signal(barrier, inc=1, device_id=peer, device_id_type=MESH)

    def greet(side):
        for cc in range(2):
            pl.semaphore_signal(barrier, inc=1, device_id=(at(side, x, cc), blk), device_id_type=MESH)

    beside(greet)
    pl.semaphore_wait(barrier, len(peers) + 4 - 2 * ends)

    def tell(s):
        def signal(side):
            pl.semaphore_signal(known.at[s], inc=1, device_id=(at(side, x, c), blk), device_id_type=MESH)

        beside(signal)

    def stage(s):
        pl.semaphore_wait(known.at[s], 2 - ends)
        if s + 1 < depth - 2:
            tell(s + 1)

    def remote(src, dst, send, recv, peer):
        return pltpu.make_async_remote_copy(
            src_ref=src, dst_ref=dst, send_sem=send, recv_sem=recv, device_id=peer, device_id_type=MESH
        )

    sent = []

    def send(*what):
        copy = remote(*what)
        copy.start()
        sent.append(copy)

    def await_recv(dst, sem):
        remote(dst, dst, wx_send.at[0, 0, 0], sem, xpeer).wait_recv()

    for p in range(PARTS):
        for b in range(1, nblk):
            send(
                q_hbm.at[:, :, pcols[p]], qbuf.at[back(b), :, :, pcols[p]],
                q_send.at[p, b], q_recv.at[p, back(b)], member(0, 0, b),
            )

    def wdst(n, source):
        return wbuf.at[pl.ds(pl.multiple_of(source * rows_w, rows_w), rows_w), pl.ds(n * chunk, chunk)]

    def wsrc(n, zz, cc):
        return w_hbm.at[:, columns(zz, blk, cc, n)]

    own_w = []
    for n in range(pieces):
        send(wsrc(n, z, c), wdst(n, req), wx_send.at[n, 0, 0], w_recv.at[n, req], xpeer)
        copy = pltpu.make_async_copy(wsrc(n, z, c), wdst(n, req), w_recv.at[n, req])
        copy.start()
        own_w.append(copy)

    rest = [(n, d) for n, d in ORDER if n < pieces and d < depth]
    rest += [(n, d) for n in range(pieces) for d in range(1, depth) if (n, d) not in rest]
    puts = [(n, 0, 1) for n in range(pieces)] + [(n, d, e) for n, d in rest for e in range(2)]
    order = [(n, d) for n, d in STEPS if n < pieces and d < depth]
    order += [pair for pair in rest if pair not in order]
    steps = [(n, 0, 1) for n in range(pieces)] + [(n, d, e) for n, d in order for e in range(2)]
    done, gone = [0], [0]

    def pump(upto):
        while gone[0] < min(upto, len(puts)):
            n, d, e = puts[gone[0]]
            gone[0] += 1
            zz, cc = flip(z, d), flip(c, e)
            send(wsrc(n, zz, cc), wdst(n, req), wz_send.at[n, d, e], w_recv.at[n, req], (at(zz, x, cc), blk))

    pump(pieces + 2 * sum(d == 1 for _, d in rest[:NEAR]))
    if depth > 2:
        tell(0)

    def forward(upto):
        while done[0] < min(upto, len(steps)):
            n, d, e = steps[done[0]]
            done[0] += 1
            source = at(flip(z, d), x, flip(c, e))
            await_recv(wdst(n, source), w_recv.at[n, source])
            send(wdst(n, source), wdst(n, source), wx_send.at[n, d, e], w_recv.at[n, source], xpeer)

    row_i = lax.broadcasted_iota(jnp.int32, (tree, tree), 0)
    col_i = lax.broadcasted_iota(jnp.int32, (tree, tree), 1)
    pick = (
        lax.broadcasted_iota(jnp.int32, (tree, own), 0)
        == lax.broadcasted_iota(jnp.int32, (tree, own), 1) + blk * own
    ).astype(jnp.float32).astype(jnp.bfloat16)
    links = [
        ((par_ref[pl.ds(r, 1), :] == row_i) | (row_i == col_i)).astype(jnp.float32) for r in range(batch)
    ]
    for _ in range((tree - 1).bit_length()):
        links = [half.astype(jnp.bfloat16) for half in links]
        links = [jnp.minimum(jnp.dot(half, half, preferred_element_type=jnp.float32), 1.0) for half in links]
    for r in range(batch):
        vtmp[r] = lax.dot_general(
            links[r].astype(jnp.bfloat16), pick, (((0,), (0,)), ((), ())),
            preferred_element_type=jnp.float32,
        )
    for r in range(batch):
        for b in range(nblk):
            there = pl.ds(pl.multiple_of(lax.rem(blk + b, nblk) * own, own), own)
            vis[r, pl.ds(b * own, own)] = vtmp[r, there]
    stat[...] = jnp.zeros_like(stat)
    for s in range(depth - 2):
        stage(s)
    pump(FIRST)

    at_key = lax.broadcasted_iota(jnp.int32, (1, keys), 1) + blk * keys
    seen = [at_key < len_ref[r] for r in range(batch)]
    lane = lax.broadcasted_iota(jnp.int32, (rows, 128), 1)
    per_p = HEADS // PARTS

    def head(p, i):
        cols = pl.ds((p * per_p + i) * HEAD, HEAD)
        stats = []
        for r in range(batch):
            tokens = [qbuf[b, r, :, cols] for b in range(nblk)]
            if own % 16:
                q = jnp.concatenate([piece.astype(jnp.float32) for piece in tokens], axis=0)
                q = q.astype(jnp.bfloat16)
            else:
                q = jnp.concatenate(tokens, axis=0)
            dims = (((1,), (1,)), ((), ()))
            s1 = lax.dot_general(q, kbuf[r, :, cols], dims, preferred_element_type=jnp.float32)
            s2 = lax.dot_general(q, dkbuf[r, :, cols], dims, preferred_element_type=jnp.float32)
            s1 = jnp.where(seen[r], s1, NEG)
            s2 = jnp.where(vis[r] > 0.5, s2, NEG)
            top = jnp.maximum(
                jnp.max(s1, axis=-1, keepdims=True), jnp.max(s2, axis=-1, keepdims=True)
            )
            top = jnp.maximum(top, 0.1 * NEG)
            p1 = jnp.exp2((s1 - top) * COEF)
            p2 = jnp.exp2((s2 - top) * COEF)
            total = jnp.sum(p1, axis=-1, keepdims=True) + jnp.sum(p2, axis=-1, keepdims=True)
            numer = jnp.dot(
                p1.astype(jnp.bfloat16), vbuf[r, :, cols], preferred_element_type=jnp.float32
            ) + jnp.dot(
                p2.astype(jnp.bfloat16), dvbuf[r, :, cols], preferred_element_type=jnp.float32
            )
            stats.append((top, total, numer))
        for b in range(nblk):
            of = slice(b * own, (b + 1) * own)
            top, total, numer = (
                jnp.concatenate([s[j][of] for s in stats], axis=0) for j in range(3)
            )
            nown[b, :, cols] = numer
            nsend[b, :, cols] = numer.astype(jnp.bfloat16)
            at_rows = pl.ds(b * rows, rows)
            stat[p, at_rows] = jnp.where(
                lane == i, top, jnp.where(lane == i + per_p, total, stat[p, at_rows])
            )

    def attend(p, half):
        if half == 0:
            for copy in kv[p]:
                copy.wait()
            for b in range(1, nblk):
                await_recv(qbuf.at[b, :, :, pcols[p]], q_recv.at[p, b])
        for i in range(half * per_p // 2, (half + 1) * per_p // 2):
            head(p, i)

    def exchange(p):
        for b in range(1, nblk):
            send(
                nsend.at[:, :, pcols[p]], nrecv.at[back(b), :, :, pcols[p]],
                n_send.at[p, b], n_recv.at[p, back(b)], member(0, 0, b),
            )
        ssend[p] = stat[p].T[: 2 * per_p]
        for b in range(1, nblk):
            send(ssend.at[p], srecv.at[p, back(b)], s_send.at[p, b], s_recv.at[p, back(b)], member(0, 0, b))

    def piece(zr, cr, yr, p):
        if yr is None:
            return abuf.at[pl.ds(slot(zr, cr, 0), nblk), :, pcols[p]]
        return abuf.at[slot(zr, cr, yr), :, pcols[p]]

    def sem(zr, cr, yr, p):
        return a_recv.at[p, slot(zr, cr, yr or 0)]

    def share(p, mine, there, to, s):
        send(piece(*mine, p), piece(*there, p), a_send.at[p, s], sem(*there, p), member(*to))

    def merge(p):
        stats = [stat[p]]
        for a in range(1, nblk):
            await_recv(nrecv.at[a, :, :, pcols[p]], n_recv.at[p, a])
            await_recv(srecv.at[p, a], s_recv.at[p, a])
            stats.append(srecv[p, a].T)
        for b in range(nblk):
            places = [(b - a) % nblk for a in range(nblk)]
            own_stats = [s[k * rows : (k + 1) * rows] for s, k in zip(stats, places)]
            tops = [s[:, :per_p] for s in own_stats]
            sums = [s[:, per_p : 2 * per_p] for s in own_stats]
            top = functools.reduce(jnp.maximum, tops)
            factors = [jnp.exp2((t - top) * COEF) for t in tops]
            total = sum(s * f for s, f in zip(sums, factors))
            factors = [f / total for f in factors]
            for i in range(per_p):
                cols = pl.ds((p * per_p + i) * HEAD, HEAD)
                row = nown[b, :, cols] * factors[0][:, i : i + 1]
                for a in range(1, nblk):
                    row = row + nrecv[a, places[a], :, cols].astype(jnp.float32) * factors[a][:, i : i + 1]
                abuf[b, :, cols] = row.astype(jnp.bfloat16)
            if b == 0 and p in PASSED:
                share(p, (0, 0, 0), (1, 0, 0), (1, 0, 0), 0)
        if p not in PASSED:
            share(p, (0, 0, None), (1, 0, None), (1, 0, 0), 0)
        share(p, (0, 0, None), (0, 1, None), (0, 1, 0), 1)

    def near(p):
        yr = 0 if p in PASSED else None
        await_recv(piece(1, 0, yr, p), sem(1, 0, yr, p))
        if p in PASSED:
            for b in range(1, nblk):
                share(p, (1, 0, 0), (1, 0, back(b)), (0, 0, b), 2 + b)
        share(p, (1, 0, yr), (1, 1, yr), (0, 1, 0), 2)

    def far(p):
        if p in PASSED:
            for b in range(1, nblk):
                await_recv(piece(1, 0, b, p), sem(1, 0, b, p))
                share(p, (1, 0, b), (1, 1, b), (0, 1, 0), 2 + nblk + b)

    for copy in locals_d:
        copy.wait()

    ymembers = [(cr, yr) for cr in range(2) for yr in range(nblk)]

    def project(n, zr):
        cols = pl.ds(n * chunk, chunk)
        out = jnp.dot(
            abuf[pl.ds(zr * 2 * nblk, 2 * nblk)].reshape(2 * nblk * rows, width), wbuf[:, cols],
            preferred_element_type=jnp.float32,
        )
        obuf[pl.ds(zr * 2 * nblk, 2 * nblk), :, :, cols] = out.reshape(2 * nblk, batch, own, chunk).astype(jnp.bfloat16)
        there = columns(z, blk, c, n)
        for cr, yr in ymembers:
            k = slot(zr, cr, yr)
            if k:
                to = slot(zr, cr, back(yr))
                send(
                    obuf.at[k, :, :, cols], out_hbm.at[:, :, there],
                    o_send.at[n, k], o_recv.at[n, to], member(zr, cr, yr),
                )
            else:
                home = pltpu.make_async_copy(obuf.at[0, :, :, cols], out_hbm.at[:, :, there], o_recv.at[n, 0])
                home.start()
                homes.append(home)

    homes = []
    ready = set()

    def finish(n, zr):
        if n >= pieces:
            return
        if zr == 0:
            pump(len(puts))
            forward(1 + max(k for k, step in enumerate(steps) if step[0] == n))
            own_w[n].wait()
            for d in range(depth):
                for e in range(2):
                    source = at(flip(z, d), 1 - x, flip(c, e))
                    await_recv(wdst(n, source), w_recv.at[n, source])
        if n == 0:
            for p in range(PARTS):
                for yr in range(nblk) if zr and p in PASSED else (None,):
                    await_recv(piece(zr, 1, yr, p), sem(zr, 1, yr, p))
        project(n, zr)

    for op in SCHEDULE:
        kind, a, b = op[0], int(op[1:] or 0), int(op[-1:] if op[1:] else 0)
        if kind == "a":
            attend(a // 10, b)
        elif kind == "e":
            exchange(a)
        elif kind == "m":
            merge(a)
        elif kind == "z":
            near(a)
        elif kind == "f":
            far(a)
        elif kind == "s":
            pump(gone[0] + 1)
        elif kind == "w":
            forward(done[0] + 1)
        else:
            finish(a // 10, b)
    for n in range(pieces):
        homes[n].wait()
        for zr in range(2):
            for cr, yr in ymembers:
                k = slot(zr, cr, yr)
                if k:
                    there = columns(flip(z, zr), lax.rem(blk + yr, nblk), flip(c, cr), n)
                    await_recv(out_hbm.at[:, :, there], o_recv.at[n, k])
    for copy in sent:
        copy.wait_send()


def shards(nreq, nblk, queries, cache_keys, cache_values, draft_keys, draft_values, parents, lengths, out_weight):
    batch, own, width = queries.shape
    keys = cache_keys.shape[1]
    tree = own * nblk
    rows = batch * own
    rows_w, model = out_weight.shape
    group = 4 * nblk
    ncols = model // group
    pieces = ncols // min(CHUNK, ncols)
    depth = nreq // LOW
    bf16, f32 = jnp.bfloat16, jnp.float32
    dma = pltpu.SemaphoreType.DMA
    hbm = pl.BlockSpec(memory_space=pltpu.HBM)
    vmem = pl.BlockSpec(memory_space=pltpu.VMEM)
    smem = pl.BlockSpec(memory_space=pltpu.SMEM)
    return pl.pallas_call(
        functools.partial(kernel, nreq, nblk),
        out_shape=jax.ShapeDtypeStruct((batch, own, model), bf16),
        in_specs=[hbm, hbm, hbm, hbm, hbm, vmem, smem, hbm],
        out_specs=hbm,
        scratch_shapes=[
            pltpu.VMEM((nblk, batch, own, width), bf16),
            pltpu.VMEM((batch, keys, width), bf16),
            pltpu.VMEM((batch, keys, width), bf16),
            pltpu.VMEM((batch, own, width), bf16),
            pltpu.VMEM((batch, own, width), bf16),
            pltpu.VMEM((batch, tree, own), f32),
            pltpu.VMEM((batch, tree, own), f32),
            pltpu.VMEM((nblk, rows, width), f32),
            pltpu.VMEM((nblk, rows, width), bf16),
            pltpu.VMEM((nblk, nblk, rows, width), bf16),
            pltpu.VMEM((PARTS, batch * tree, 128), f32),
            pltpu.VMEM((PARTS, 2 * HEADS // PARTS, batch * tree), f32),
            pltpu.VMEM((PARTS, nblk, 2 * HEADS // PARTS, batch * tree), f32),
            pltpu.VMEM((group, rows, width), bf16),
            pltpu.VMEM((rows_w * nreq, ncols), bf16),
            pltpu.VMEM((group, batch, own, ncols), bf16),
            dma((2, PARTS)),
            dma((3,)),
            dma((PARTS, nblk)),
            dma((PARTS, nblk)),
            dma((PARTS, nblk)),
            dma((PARTS, nblk)),
            dma((PARTS, nblk)),
            dma((PARTS, nblk)),
            dma((pieces, depth, 2)),
            dma((pieces, depth, 2)),
            dma((pieces, nreq)),
            pltpu.SemaphoreType.REGULAR((depth - 2,)),
            dma((PARTS, 2 + 4 * nblk)),
            dma((PARTS, group)),
            dma((pieces, group)),
            dma((pieces, group)),
        ],
        compiler_params=pltpu.CompilerParams(
            collective_id=0, has_side_effects=True, vmem_limit_bytes=58 * 1024 * 1024
        ),
    )(queries, cache_keys, cache_values, draft_keys, draft_values, parents, lengths, out_weight)


def solution(mesh):
    in_specs = (
        P("req", "blk", None),
        P("req", "blk", None),
        P("req", "blk", None),
        P("req", "blk", None),
        P("req", "blk", None),
        P("req", None),
        P("req"),
        P("req", None),
    )
    out_specs = P("req", "blk", None)
    body = functools.partial(shards, mesh.shape["req"], mesh.shape["blk"])
    return jax.shard_map(body, mesh=mesh, in_specs=in_specs, out_specs=out_specs, check_vma=False)
```

```python
import functools

import jax
import jax.numpy as jnp
from jax import lax
from jax.experimental import pallas as pl
from jax.experimental.pallas import tpu as pltpu
from jax.sharding import PartitionSpec as P

HEAD = 128
HEADS = 16
LOW = 4
PARTS = 4
CHUNK = 256
FIRST = 14
NEAR = 2
ORDER = ((0, 1), (1, 1), (0, 2), (0, 3), (1, 2), (1, 3), )
STEPS = ((0, 1), (1, 1), (0, 2), (0, 3), (1, 2), (1, 3), )
PASSED = (0, 1, )
SCHEDULE = ("a00", "a01", "w", "w", "e0", "a10", "a11", "w", "w", "e1", "w", "w", "m0", "a20", "a21", "e2", "m1", "w", "a30", "a31", "e3", "w", "m2", "z0", "w", "m3", "w", "z1", "w", "w", "f0", "z2", "w", "f1", "w", "z3", "p00", "p01", "p10", "p11",)
MESH = pl.DeviceIdType.MESH
NEG = -1e30
COEF = HEAD**-0.5 * 1.4426950408889634


def flip(value, bits):
    out = value
    bit = 1
    while bit <= bits:
        if bits & bit:
            out = out + bit - 2 * bit * ((value // bit) % 2)
        bit *= 2
    return out


def kernel(
    nreq, nblk,
    q_hbm, ck_hbm, cv_hbm, dk_hbm, dv_hbm, par_ref, len_ref, w_hbm,
    out_hbm,
    qbuf, kbuf, vbuf, dkbuf, dvbuf, vtmp, vis, nown, nsend, nrecv, stat, ssend, srecv, abuf, wbuf, obuf,
    kv_sem, d_sem, q_send, q_recv, n_send, n_recv, s_send, s_recv,
    wz_send, wx_send, w_recv, known, a_send, a_recv, o_send, o_recv,
):
    batch, own, width = q_hbm.shape
    keys = ck_hbm.shape[1]
    tree = own * nblk
    rows = batch * own
    rows_w, model = w_hbm.shape
    ncols = model // (4 * nblk)
    chunk = min(CHUNK, ncols)
    pieces = ncols // chunk
    depth = nreq // LOW
    req, blk = lax.axis_index("req"), lax.axis_index("blk")
    z, x, c = req // LOW, (req // 2) % 2, req % 2

    def at(zz, xx, cc):
        return zz * LOW + xx * 2 + cc

    def slot(zr, cr, yr):
        return (zr * 2 + cr) * nblk + yr

    def member(zr, cr, yr):
        return (at(flip(z, zr), x, flip(c, cr)), lax.rem(blk + yr, nblk))

    def columns(zz, yy, cc, n):
        index = ((zz % 2) * nblk + yy) * 2 + cc
        return pl.ds(pl.multiple_of(index * ncols + n * chunk, chunk), chunk)

    def back(yr):
        return (nblk - yr) % nblk

    part = width // PARTS
    pcols = [pl.ds(p * part, part) for p in range(PARTS)]

    locals_d = [
        pltpu.make_async_copy(q_hbm, qbuf.at[0], d_sem.at[0]),
        pltpu.make_async_copy(dk_hbm, dkbuf, d_sem.at[1]),
        pltpu.make_async_copy(dv_hbm, dvbuf, d_sem.at[2]),
    ]
    for copy in locals_d:
        copy.start()
    kv = []
    for p in range(PARTS):
        pair = (
            pltpu.make_async_copy(ck_hbm.at[:, :, pcols[p]], kbuf.at[:, :, pcols[p]], kv_sem.at[0, p]),
            pltpu.make_async_copy(cv_hbm.at[:, :, pcols[p]], vbuf.at[:, :, pcols[p]], kv_sem.at[1, p]),
        )
        for copy in pair:
            copy.start()
        kv.append(pair)

    xpeer = (at(z, 1 - x, c), blk)
    line = [(d, e) for d in range(depth) for e in range(2) if d or e]
    peers = [xpeer, (at(z, x, 1 - c), blk)] + [member(0, 0, b) for b in range(1, nblk)]
    barrier = pltpu.get_barrier_semaphore()

    def beside(act):
        for side, exists in ((z - 1, z > 0), (z + 1, z < depth - 1)):
            @pl.when(exists)
            def _():
                act(side)

    ends = (z == 0).astype(jnp.int32) + (z == depth - 1).astype(jnp.int32)
    for peer in peers:
        pl.semaphore_signal(barrier, inc=1, device_id=peer, device_id_type=MESH)

    def greet(side):
        for cc in range(2):
            pl.semaphore_signal(barrier, inc=1, device_id=(at(side, x, cc), blk), device_id_type=MESH)

    beside(greet)
    pl.semaphore_wait(barrier, len(peers) + 4 - 2 * ends)

    def tell(s):
        def signal(side):
            pl.semaphore_signal(known.at[s], inc=1, device_id=(at(side, x, c), blk), device_id_type=MESH)

        beside(signal)

    def stage(s):
        pl.semaphore_wait(known.at[s], 2 - ends)
        if s + 1 < depth - 2:
            tell(s + 1)

    def remote(src, dst, send, recv, peer):
        return pltpu.make_async_remote_copy(
            src_ref=src, dst_ref=dst, send_sem=send, recv_sem=recv, device_id=peer, device_id_type=MESH
        )

    sent = []

    def send(*what):
        copy = remote(*what)
        copy.start()
        sent.append(copy)

    def await_recv(dst, sem):
        remote(dst, dst, wx_send.at[0, 0, 0], sem, xpeer).wait_recv()

    for p in range(PARTS):
        for b in range(1, nblk):
            send(
                q_hbm.at[:, :, pcols[p]], qbuf.at[back(b), :, :, pcols[p]],
                q_send.at[p, b], q_recv.at[p, back(b)], member(0, 0, b),
            )

    def wdst(n, source):
        return wbuf.at[pl.ds(pl.multiple_of(source * rows_w, rows_w), rows_w), pl.ds(n * chunk, chunk)]

    def wsrc(n, zz, cc):
        return w_hbm.at[:, columns(zz, blk, cc, n)]

    own_w = []
    for n in range(pieces):
        send(wsrc(n, z, c), wdst(n, req), wx_send.at[n, 0, 0], w_recv.at[n, req], xpeer)
        copy = pltpu.make_async_copy(wsrc(n, z, c), wdst(n, req), w_recv.at[n, req])
        copy.start()
        own_w.append(copy)

    rest = [(n, d) for n, d in ORDER if n < pieces and d < depth]
    rest += [(n, d) for n in range(pieces) for d in range(1, depth) if (n, d) not in rest]
    puts = [(n, 0, 1) for n in range(pieces)] + [(n, d, e) for n, d in rest for e in range(2)]
    order = [(n, d) for n, d in STEPS if n < pieces and d < depth]
    order += [pair for pair in rest if pair not in order]
    steps = [(n, 0, 1) for n in range(pieces)] + [(n, d, e) for n, d in order for e in range(2)]
    done, gone = [0], [0]

    def pump(upto):
        while gone[0] < min(upto, len(puts)):
            n, d, e = puts[gone[0]]
            gone[0] += 1
            zz, cc = flip(z, d), flip(c, e)
            send(wsrc(n, zz, cc), wdst(n, req), wz_send.at[n, d, e], w_recv.at[n, req], (at(zz, x, cc), blk))

    pump(pieces + 2 * sum(d == 1 for _, d in rest[:NEAR]))
    if depth > 2:
        tell(0)

    def forward(upto):
        while done[0] < min(upto, len(steps)):
            n, d, e = steps[done[0]]
            done[0] += 1
            source = at(flip(z, d), x, flip(c, e))
            await_recv(wdst(n, source), w_recv.at[n, source])
            send(wdst(n, source), wdst(n, source), wx_send.at[n, d, e], w_recv.at[n, source], xpeer)

    row_i = lax.broadcasted_iota(jnp.int32, (tree, tree), 0)
    col_i = lax.broadcasted_iota(jnp.int32, (tree, tree), 1)
    pick = (
        lax.broadcasted_iota(jnp.int32, (tree, own), 0)
        == lax.broadcasted_iota(jnp.int32, (tree, own), 1) + blk * own
    ).astype(jnp.float32).astype(jnp.bfloat16)
    links = [
        ((par_ref[pl.ds(r, 1), :] == row_i) | (row_i == col_i)).astype(jnp.float32) for r in range(batch)
    ]
    for _ in range((tree - 1).bit_length()):
        links = [half.astype(jnp.bfloat16) for half in links]
        links = [jnp.minimum(jnp.dot(half, half, preferred_element_type=jnp.float32), 1.0) for half in links]
    for r in range(batch):
        vtmp[r] = lax.dot_general(
            links[r].astype(jnp.bfloat16), pick, (((0,), (0,)), ((), ())),
            preferred_element_type=jnp.float32,
        )
    for r in range(batch):
        for b in range(nblk):
            there = pl.ds(pl.multiple_of(lax.rem(blk + b, nblk) * own, own), own)
            vis[r, pl.ds(b * own, own)] = vtmp[r, there]
    stat[...] = jnp.zeros_like(stat)
    for s in range(depth - 2):
        stage(s)
    pump(FIRST)

    at_key = lax.broadcasted_iota(jnp.int32, (1, keys), 1) + blk * keys
    seen = [at_key < len_ref[r] for r in range(batch)]
    lane = lax.broadcasted_iota(jnp.int32, (rows, 128), 1)
    per_p = HEADS // PARTS

    def head(p, i):
        cols = pl.ds((p * per_p + i) * HEAD, HEAD)
        stats = []
        for r in range(batch):
            tokens = [qbuf[b, r, :, cols] for b in range(nblk)]
            if own % 16:
                q = jnp.concatenate([piece.astype(jnp.float32) for piece in tokens], axis=0)
                q = q.astype(jnp.bfloat16)
            else:
                q = jnp.concatenate(tokens, axis=0)
            dims = (((1,), (1,)), ((), ()))
            s1 = lax.dot_general(q, kbuf[r, :, cols], dims, preferred_element_type=jnp.float32)
            s2 = lax.dot_general(q, dkbuf[r, :, cols], dims, preferred_element_type=jnp.float32)
            s1 = jnp.where(seen[r], s1, NEG)
            s2 = jnp.where(vis[r] > 0.5, s2, NEG)
            top = jnp.maximum(
                jnp.max(s1, axis=-1, keepdims=True), jnp.max(s2, axis=-1, keepdims=True)
            )
            top = jnp.maximum(top, 0.1 * NEG)
            p1 = jnp.exp2((s1 - top) * COEF)
            p2 = jnp.exp2((s2 - top) * COEF)
            total = jnp.sum(p1, axis=-1, keepdims=True) + jnp.sum(p2, axis=-1, keepdims=True)
            numer = jnp.dot(
                p1.astype(jnp.bfloat16), vbuf[r, :, cols], preferred_element_type=jnp.float32
            ) + jnp.dot(
                p2.astype(jnp.bfloat16), dvbuf[r, :, cols], preferred_element_type=jnp.float32
            )
            stats.append((top, total, numer))
        for b in range(nblk):
            of = slice(b * own, (b + 1) * own)
            top, total, numer = (
                jnp.concatenate([s[j][of] for s in stats], axis=0) for j in range(3)
            )
            nown[b, :, cols] = numer
            nsend[b, :, cols] = numer.astype(jnp.bfloat16)
            at_rows = pl.ds(b * rows, rows)
            stat[p, at_rows] = jnp.where(
                lane == i, top, jnp.where(lane == i + per_p, total, stat[p, at_rows])
            )

    def attend(p, half):
        if half == 0:
            for copy in kv[p]:
                copy.wait()
            for b in range(1, nblk):
                await_recv(qbuf.at[b, :, :, pcols[p]], q_recv.at[p, b])
        for i in range(half * per_p // 2, (half + 1) * per_p // 2):
            head(p, i)

    def exchange(p):
        for b in range(1, nblk):
            send(
                nsend.at[:, :, pcols[p]], nrecv.at[back(b), :, :, pcols[p]],
                n_send.at[p, b], n_recv.at[p, back(b)], member(0, 0, b),
            )
        ssend[p] = stat[p].T[: 2 * per_p]
        for b in range(1, nblk):
            send(ssend.at[p], srecv.at[p, back(b)], s_send.at[p, b], s_recv.at[p, back(b)], member(0, 0, b))

    def piece(zr, cr, yr, p):
        if yr is None:
            return abuf.at[pl.ds(slot(zr, cr, 0), nblk), :, pcols[p]]
        return abuf.at[slot(zr, cr, yr), :, pcols[p]]

    def sem(zr, cr, yr, p):
        return a_recv.at[p, slot(zr, cr, yr or 0)]

    def share(p, mine, there, to, s):
        send(piece(*mine, p), piece(*there, p), a_send.at[p, s], sem(*there, p), member(*to))

    def merge(p):
        stats = [stat[p]]
        for a in range(1, nblk):
            await_recv(nrecv.at[a, :, :, pcols[p]], n_recv.at[p, a])
            await_recv(srecv.at[p, a], s_recv.at[p, a])
            stats.append(srecv[p, a].T)
        for b in range(nblk):
            places = [(b - a) % nblk for a in range(nblk)]
            own_stats = [s[k * rows : (k + 1) * rows] for s, k in zip(stats, places)]
            tops = [s[:, :per_p] for s in own_stats]
            sums = [s[:, per_p : 2 * per_p] for s in own_stats]
            top = functools.reduce(jnp.maximum, tops)
            factors = [jnp.exp2((t - top) * COEF) for t in tops]
            total = sum(s * f for s, f in zip(sums, factors))
            factors = [f / total for f in factors]
            for i in range(per_p):
                cols = pl.ds((p * per_p + i) * HEAD, HEAD)
                row = nown[b, :, cols] * factors[0][:, i : i + 1]
                for a in range(1, nblk):
                    row = row + nrecv[a, places[a], :, cols].astype(jnp.float32) * factors[a][:, i : i + 1]
                abuf[b, :, cols] = row.astype(jnp.bfloat16)
            if b == 0 and p in PASSED:
                share(p, (0, 0, 0), (1, 0, 0), (1, 0, 0), 0)
            if p not in PASSED:
                share(p, (0, 0, b), (1, 0, b), (1, 0, 0), 2 + 2 * nblk + b)
        share(p, (0, 0, None), (0, 1, None), (0, 1, 0), 1)

    def near(p):
        if p not in PASSED:
            for b in range(nblk):
                await_recv(piece(1, 0, b, p), sem(1, 0, b, p))
                share(p, (1, 0, b), (1, 1, b), (0, 1, 0), 2 + 3 * nblk + b)
            return
        await_recv(piece(1, 0, 0, p), sem(1, 0, 0, p))
        if p in PASSED:
            for b in range(1, nblk):
                share(p, (1, 0, 0), (1, 0, back(b)), (0, 0, b), 2 + b)
        share(p, (1, 0, 0), (1, 1, 0), (0, 1, 0), 2)

    def far(p):
        if p in PASSED:
            for b in range(1, nblk):
                await_recv(piece(1, 0, b, p), sem(1, 0, b, p))
                share(p, (1, 0, b), (1, 1, b), (0, 1, 0), 2 + nblk + b)

    for copy in locals_d:
        copy.wait()

    ymembers = [(cr, yr) for cr in range(2) for yr in range(nblk)]

    def project(n, zr):
        cols = pl.ds(n * chunk, chunk)
        out = jnp.dot(
            abuf[pl.ds(zr * 2 * nblk, 2 * nblk)].reshape(2 * nblk * rows, width), wbuf[:, cols],
            preferred_element_type=jnp.float32,
        )
        obuf[pl.ds(zr * 2 * nblk, 2 * nblk), :, :, cols] = out.reshape(2 * nblk, batch, own, chunk).astype(jnp.bfloat16)
        there = columns(z, blk, c, n)
        for cr, yr in ymembers:
            k = slot(zr, cr, yr)
            if k:
                to = slot(zr, cr, back(yr))
                send(
                    obuf.at[k, :, :, cols], out_hbm.at[:, :, there],
                    o_send.at[n, k], o_recv.at[n, to], member(zr, cr, yr),
                )
            else:
                home = pltpu.make_async_copy(obuf.at[0, :, :, cols], out_hbm.at[:, :, there], o_recv.at[n, 0])
                home.start()
                homes.append(home)

    homes = []
    ready = set()

    def finish(n, zr):
        if n >= pieces:
            return
        if zr == 0:
            pump(len(puts))
            forward(1 + max(k for k, step in enumerate(steps) if step[0] == n))
            own_w[n].wait()
            for d in range(depth):
                for e in range(2):
                    source = at(flip(z, d), 1 - x, flip(c, e))
                    await_recv(wdst(n, source), w_recv.at[n, source])
        if n == 0:
            for p in range(PARTS):
                for yr in range(nblk) if zr else (None,):
                    await_recv(piece(zr, 1, yr, p), sem(zr, 1, yr, p))
        project(n, zr)

    for op in SCHEDULE:
        kind, a, b = op[0], int(op[1:] or 0), int(op[-1:] if op[1:] else 0)
        if kind == "a":
            attend(a // 10, b)
        elif kind == "e":
            exchange(a)
        elif kind == "m":
            merge(a)
        elif kind == "z":
            near(a)
        elif kind == "f":
            far(a)
        elif kind == "s":
            pump(gone[0] + 1)
        elif kind == "w":
            forward(done[0] + 1)
        else:
            finish(a // 10, b)
    for n in range(pieces):
        homes[n].wait()
        for zr in range(2):
            for cr, yr in ymembers:
                k = slot(zr, cr, yr)
                if k:
                    there = columns(flip(z, zr), lax.rem(blk + yr, nblk), flip(c, cr), n)
                    await_recv(out_hbm.at[:, :, there], o_recv.at[n, k])
    for copy in sent:
        copy.wait_send()


def shards(nreq, nblk, queries, cache_keys, cache_values, draft_keys, draft_values, parents, lengths, out_weight):
    batch, own, width = queries.shape
    keys = cache_keys.shape[1]
    tree = own * nblk
    rows = batch * own
    rows_w, model = out_weight.shape
    group = 4 * nblk
    ncols = model // group
    pieces = ncols // min(CHUNK, ncols)
    depth = nreq // LOW
    bf16, f32 = jnp.bfloat16, jnp.float32
    dma = pltpu.SemaphoreType.DMA
    hbm = pl.BlockSpec(memory_space=pltpu.HBM)
    vmem = pl.BlockSpec(memory_space=pltpu.VMEM)
    smem = pl.BlockSpec(memory_space=pltpu.SMEM)
    return pl.pallas_call(
        functools.partial(kernel, nreq, nblk),
        out_shape=jax.ShapeDtypeStruct((batch, own, model), bf16),
        in_specs=[hbm, hbm, hbm, hbm, hbm, vmem, smem, hbm],
        out_specs=hbm,
        scratch_shapes=[
            pltpu.VMEM((nblk, batch, own, width), bf16),
            pltpu.VMEM((batch, keys, width), bf16),
            pltpu.VMEM((batch, keys, width), bf16),
            pltpu.VMEM((batch, own, width), bf16),
            pltpu.VMEM((batch, own, width), bf16),
            pltpu.VMEM((batch, tree, own), f32),
            pltpu.VMEM((batch, tree, own), f32),
            pltpu.VMEM((nblk, rows, width), f32),
            pltpu.VMEM((nblk, rows, width), bf16),
            pltpu.VMEM((nblk, nblk, rows, width), bf16),
            pltpu.VMEM((PARTS, batch * tree, 128), f32),
            pltpu.VMEM((PARTS, 2 * HEADS // PARTS, batch * tree), f32),
            pltpu.VMEM((PARTS, nblk, 2 * HEADS // PARTS, batch * tree), f32),
            pltpu.VMEM((group, rows, width), bf16),
            pltpu.VMEM((rows_w * nreq, ncols), bf16),
            pltpu.VMEM((group, batch, own, ncols), bf16),
            dma((2, PARTS)),
            dma((3,)),
            dma((PARTS, nblk)),
            dma((PARTS, nblk)),
            dma((PARTS, nblk)),
            dma((PARTS, nblk)),
            dma((PARTS, nblk)),
            dma((PARTS, nblk)),
            dma((pieces, depth, 2)),
            dma((pieces, depth, 2)),
            dma((pieces, nreq)),
            pltpu.SemaphoreType.REGULAR((depth - 2,)),
            dma((PARTS, 2 + 4 * nblk)),
            dma((PARTS, group)),
            dma((pieces, group)),
            dma((pieces, group)),
        ],
        compiler_params=pltpu.CompilerParams(
            collective_id=0, has_side_effects=True, vmem_limit_bytes=58 * 1024 * 1024
        ),
    )(queries, cache_keys, cache_values, draft_keys, draft_values, parents, lengths, out_weight)


def solution(mesh):
    in_specs = (
        P("req", "blk", None),
        P("req", "blk", None),
        P("req", "blk", None),
        P("req", "blk", None),
        P("req", "blk", None),
        P("req", None),
        P("req"),
        P("req", None),
    )
    out_specs = P("req", "blk", None)
    body = functools.partial(shards, mesh.shape["req"], mesh.shape["blk"])
    return jax.shard_map(body, mesh=mesh, in_specs=in_specs, out_specs=out_specs, check_vma=False)
```
